32 devices in a mesh: rows: 4 (over y, core), cols: 8 (over z, x).
Axes of the slice: x: 2, y: 2, z: 4, core: 2. Of those that a mesh axis runs over, the one named last changes fastest.
Arguments:
- iterate: bfloat16 [3584, 20480], P('rows', 'cols'), may hold values from -4.5 to 4.5
Outputs:
- updated: bfloat16 [3584, 20480], P('rows', 'cols')
The draws below stay inside these ranges and needn't reach their ends.
All inputs are finite; a program needn't handle non-finite values.
Results may differ from the reference program's by a relative error of at most 0.0054.
Values may be sent and summed in bfloat16 or wider, within the bound.
A program may use at most 128 MiB of HBM per device.

```python
import math
import jax
import jax.numpy as jnp
from jax import lax

M = 3584
V = 20480


def draw_iterate(key, part):
    key_scale = jax.random.fold_in(key, 11)
    key_entry = jax.random.fold_in(key, 12)
    key_left = jax.random.fold_in(key, 13)
    key_right = jax.random.fold_in(key, 14)
    scales = jnp.exp(jax.random.uniform(key_scale, (M, 1), jnp.float32, minval=math.log(0.1), maxval=0.0))
    left = jax.random.normal(key_left, (M, 4), jnp.float32)
    right = jax.random.normal(key_right, (4, V), jnp.float32)
    shared = left[:, 0:1] * right[0:1, :] + left[:, 1:2] * right[1:2, :]
    shared = shared + left[:, 2:3] * right[2:3, :] + left[:, 3:4] * right[3:4, :]
    strength = math.sqrt(4.0 * 0.5 / (0.215 * M))
    noise = jax.random.normal(key_entry, (M, V), jnp.float32)
    entries = jnp.clip(strength * 0.5 * shared + noise, -4.5, 4.5)
    return (scales * entries).astype(jnp.bfloat16)


def setup_inputs(seed: int = 0) -> dict:
    arg_keys = jax.random.split(jax.random.key(seed), 2)
    return {
        "iterate": draw_iterate(jax.random.fold_in(arg_keys[1], 71), 0),
    }


linear_coef = 3.4445
cubic_coef = -4.7750
quintic_coef = 2.0315


def reference(iterate):
    values = iterate.astype(jnp.float32)
    gram = (jnp.dot(values, values.T, precision=lax.Precision.HIGHEST) / V).astype(jnp.bfloat16)
    gram_wide = gram.astype(jnp.float32)
    square = jnp.dot(gram_wide, gram_wide, precision=lax.Precision.HIGHEST)
    poly_gram = (cubic_coef * gram_wide + quintic_coef * square).astype(jnp.bfloat16)
    result = linear_coef * values + jnp.dot(poly_gram.astype(jnp.float32), values, precision=lax.Precision.HIGHEST)
    return result.astype(jnp.bfloat16)
```

```python
import functools

import jax
import jax.numpy as jnp
from jax import lax
from jax.experimental import pallas as pl
from jax.experimental.pallas import tpu as pltpu
from jax.sharding import PartitionSpec as P

linear_coef = 3.4445
cubic_coef = -4.775
quintic_coef = 2.0315

MESH = pl.DeviceIdType.MESH
ANY = pl.BlockSpec(memory_space=pl.ANY)
bf16 = jnp.bfloat16


def greet(peers):
    barrier = pltpu.get_barrier_semaphore()
    for peer in peers:
        pl.semaphore_signal(barrier, inc=1, device_id=peer, device_id_type=MESH)
    pl.semaphore_wait(barrier, len(peers))


def remote(src, dst, send, recv, peer):
    return pltpu.make_async_remote_copy(
        src_ref=src, dst_ref=dst, send_sem=send, recv_sem=recv, device_id=peer, device_id_type=MESH
    )


def flip(index, bit):
    return index + bit - 2 * bit * ((index // bit) % 2)


def place():
    row, col = lax.axis_index("rows"), lax.axis_index("cols")
    return row, col


def pair_kernel(chunks, x_ref, pair_ref, send, recv, local):
    row, col = place()
    sibling = (flip(row, 1), col)
    core = row % 2
    greet([sibling])
    size = x_ref.shape[0] // chunks
    copies = []
    for j in range(chunks):
        part = pl.ds(j * size, size)
        copy = remote(x_ref.at[part], pair_ref.at[core, part], send.at[j], recv.at[j], sibling)
        copy.start()
        copies.append(copy)
    own = pltpu.make_async_copy(x_ref, pair_ref.at[core], local)
    own.start()
    for copy in copies:
        copy.wait()
    own.wait()


def start_scatter(cols, part_ref, got_ref, send, recv, local):
    row, col = place()
    copies = []
    for k in range(1, cols):
        dest = (col + k) % cols
        copy = remote(part_ref.at[dest], got_ref.at[k], send.at[k], recv.at[k], (row, dest))
        copy.start()
        copies.append(copy)
    own = pltpu.make_async_copy(part_ref.at[col], got_ref.at[0], local)
    own.start()
    copies.append(own)
    return copies


def rows_kernel(
    cols, chunks, pair_ref, part_ref, all_ref, got_ref,
    y_send, y_recv, f_send, f_recv, s_send, s_recv, local,
):
    row, col = place()
    core = row % 2
    across, sibling = (flip(row, 2), col), (flip(row, 1), col)
    greet([across, sibling] + [(row, (col + k) % cols) for k in range(1, cols)])
    size = pair_ref.shape[1] // chunks
    parts = [pl.ds(j * size, size) for j in range(chunks)]
    outgoing = []
    for j, part in enumerate(parts):
        copy = remote(
            pair_ref.at[core, part], all_ref.at[row, part], y_send.at[j], y_recv.at[j], across
        )
        copy.start()
        outgoing.append(copy)
    scatter = start_scatter(cols, part_ref, got_ref, s_send, s_recv, local.at[0])
    keep = pltpu.make_async_copy(pair_ref, all_ref.at[pl.ds(row - core, 2)], local.at[1])
    keep.start()
    forwards = []
    for j, part in enumerate(parts):
        outgoing[j].wait_recv()
        there = all_ref.at[flip(row, 2), part]
        copy = remote(there, there, f_send.at[j], f_recv.at[j], sibling)
        copy.start()
        forwards.append(copy)
    for copy in outgoing:
        copy.wait_send()
    for copy in scatter + [keep] + forwards:
        copy.wait()


def gather(rows, cols, share_ref, all_ref, send, recv, local):
    row, col = place()
    side, across, sibling = (row, flip(col, 1)), (flip(row, 2), col), (flip(row, 1), col)
    group = cols // 2
    sent = []

    def push(src, r, c, peer):
        copy = remote(src, all_ref.at[r, c], send.at[len(sent)], recv.at[r, c], peer)
        copy.start()
        sent.append(copy)

    def arrived(r, c):
        slot = all_ref.at[r, c]
        remote(slot, slot, send.at[0], recv.at[r, c], sibling).wait_recv()

    def member(m):
        return ((col // 2 + m) % group) * 2 + col % 2

    for m in range(1, group):
        push(share_ref, row, col, (row, member(group - m)))
    push(share_ref, row, col, side)
    push(share_ref, row, col, across)
    push(share_ref, row, col, sibling)
    own = pltpu.make_async_copy(share_ref, all_ref.at[row, col], local)
    own.start()
    far = flip(row, 2)
    for m in range(1, group):
        c = member(m)
        arrived(row, c)
        for peer in (side, across, sibling):
            push(all_ref.at[row, c], row, c, peer)
    for m in range(group):
        c = flip(member(m), 1)
        arrived(row, c)
        if 2 * m < group:
            push(all_ref.at[row, c], row, c, across)
        push(all_ref.at[row, c], row, c, sibling)
        c = member(m)
        arrived(far, c)
        if 2 * m >= group:
            push(all_ref.at[far, c], far, c, side)
        push(all_ref.at[far, c], far, c, sibling)
    for m in range(group):
        c = flip(member(m), 1)
        arrived(far, c)
        push(all_ref.at[far, c], far, c, sibling)
    for r in (flip(row, 1), flip(flip(row, 1), 2)):
        for c in range(cols):
            arrived(r, c)
    for copy in sent:
        copy.wait_send()
    own.wait()


def gather_sends(cols):
    group = cols // 2
    return (group - 1) + 3 + 3 * (group - 1) + 3 * group + group


def gather_peers(cols):
    row, col = place()
    return [(flip(row, 2), col), (flip(row, 1), col)] + [(row, (col + k) % cols) for k in range(1, cols)]


def both_kernel(rows, cols, part_ref, share_ref, got_ref, all_ref, s_send, s_recv, g_send, g_recv, local):
    greet(gather_peers(cols))
    scatter = start_scatter(cols, part_ref, got_ref, s_send, s_recv, local.at[0])
    gather(rows, cols, share_ref, all_ref, g_send, g_recv, local.at[1])
    for copy in scatter:
        copy.wait()


def gather_kernel(rows, cols, share_ref, all_ref, g_send, g_recv, local):
    greet(gather_peers(cols))
    gather(rows, cols, share_ref, all_ref, g_send, g_recv, local.at[0])


def call(kernel, ident, args, outs, sems):
    return pl.pallas_call(
        kernel,
        out_shape=outs,
        in_specs=[ANY] * len(args),
        out_specs=[ANY] * len(outs),
        scratch_shapes=[pltpu.SemaphoreType.DMA(shape) for shape in sems],
        compiler_params=pltpu.CompilerParams(collective_id=ident, has_side_effects=True),
    )(*args)


def dot_rows(left, right):
    return lax.dot_general(
        left, right, (((1,), (1,)), ((), ())), preferred_element_type=jnp.float32
    )


def round_up(value, unit):
    return -(-value // unit) * unit


def chunked(tile, cols):
    count = round_up(-(-tile.shape[0] // cols), 16)
    tile = jnp.pad(tile, ((0, count * cols - tile.shape[0]), (0, 0)))
    return tile.reshape(cols, count, tile.shape[1])


def on_device(iterate):
    rows, cols = lax.axis_size("rows"), lax.axis_size("cols")
    row = lax.axis_index("rows")
    block, width = iterate.shape
    half = block // 2
    vocab = width * cols
    full = block * rows
    chunks = 8

    def shape(*dims):
        return jax.ShapeDtypeStruct(dims, bf16)

    (pair,) = call(
        functools.partial(pair_kernel, 4), 1, [iterate], [shape(2, block, width)], [(4,), (4,), ()]
    )
    top = lax.dynamic_slice(pair, (0, (row % 2) * half, 0), (1, half, width))[0]
    near = jnp.concatenate(
        [dot_rows(iterate, iterate).astype(bf16), dot_rows(top, pair[1]).astype(bf16)], axis=0
    )
    near = chunked(near, cols)
    near_rows = near.shape[1]
    all_rows, got = call(
        functools.partial(rows_kernel, cols, chunks),
        2,
        [pair, near],
        [shape(rows, block, width), shape(cols, near_rows, block)],
        [(chunks,)] * 4 + [(cols,), (cols,), (2,)],
    )

    def summed(parts):
        return (jnp.sum(parts.astype(jnp.float32), axis=0) / vocab).astype(bf16)

    near_share = summed(got)
    other = jnp.where(row < 2, row + 2, rows - 1 - row)
    cross = dot_rows(iterate, lax.dynamic_index_in_dim(all_rows, other, 0, keepdims=False)).astype(bf16)
    cross = chunked(cross, cols)
    cross_rows = cross.shape[1]
    sends = gather_sends(cols)
    got, near_all = call(
        functools.partial(both_kernel, rows, cols),
        3,
        [cross, near_share],
        [shape(cols, cross_rows, block), shape(rows, cols, near_rows, block)],
        [(cols,), (cols,), (sends,), (rows, cols), (2,)],
    )
    (cross_all,) = call(
        functools.partial(gather_kernel, rows, cols),
        4,
        [summed(got)],
        [shape(rows, cols, cross_rows, block)],
        [(sends,), (rows, cols), (2,)],
    )
    near_all = near_all.reshape(rows, cols * near_rows, block)
    cross_all = cross_all.reshape(rows, cols * cross_rows, block)[:, :block]
    diag = near_all[:, :block]
    ab = near_all[0:2, block : block + half].reshape(block, block)
    cd = near_all[2:4, block : block + half].reshape(block, block)
    ac, bd, cb, da = cross_all[0], cross_all[1], cross_all[2], cross_all[3]
    gram = jnp.concatenate(
        [
            jnp.concatenate([diag[0], ab, ac, da.T], axis=1),
            jnp.concatenate([ab.T, diag[1], cb.T, bd], axis=1),
            jnp.concatenate([ac.T, cb, diag[2], cd], axis=1),
            jnp.concatenate([da, bd.T, cd.T, diag[3]], axis=1),
        ],
        axis=0,
    )
    gram_rows = lax.dynamic_slice_in_dim(gram, row * block, block, 0)
    square = jnp.dot(gram_rows, gram, preferred_element_type=jnp.float32)
    poly = (cubic_coef * gram_rows.astype(jnp.float32) + quintic_coef * square).astype(bf16)
    linear_part = linear_coef * iterate.astype(jnp.float32)
    mixed = linear_part + jnp.dot(
        poly, all_rows.reshape(full, width), preferred_element_type=jnp.float32
    )
    return mixed.astype(bf16)


def solution(mesh):
    return jax.shard_map(
        on_device,
        mesh=mesh,
        in_specs=(P("rows", "cols"),),
        out_specs=P("rows", "cols"),
        check_vma=False,
    )
```

```python
import functools

import jax
import jax.numpy as jnp
from jax import lax
from jax.experimental import pallas as pl
from jax.experimental.pallas import tpu as pltpu
from jax.sharding import PartitionSpec as P

linear_coef = 3.4445
cubic_coef = -4.775
quintic_coef = 2.0315

MESH = pl.DeviceIdType.MESH
ANY = pl.BlockSpec(memory_space=pl.ANY)
bf16 = jnp.bfloat16


def greet(peers):
    barrier = pltpu.get_barrier_semaphore()
    for peer in peers:
        pl.semaphore_signal(barrier, inc=1, device_id=peer, device_id_type=MESH)
    pl.semaphore_wait(barrier, len(peers))


def remote(src, dst, send, recv, peer):
    return pltpu.make_async_remote_copy(
        src_ref=src, dst_ref=dst, send_sem=send, recv_sem=recv, device_id=peer, device_id_type=MESH
    )


def flip(index, bit):
    return index + bit - 2 * bit * ((index // bit) % 2)


def place():
    row, col = lax.axis_index("rows"), lax.axis_index("cols")
    return row, col


def through_vmem(src, dst, held, sem):
    for a, b in ((src, held), (held, dst)):
        copy = pltpu.make_async_copy(a, b, sem)
        copy.start()
        copy.wait()


def pair_kernel(chunks, x_ref, pair_ref, send, recv, local, held):
    row, col = place()
    sibling = (flip(row, 1), col)
    core = row % 2
    greet([sibling])
    size = x_ref.shape[0] // chunks
    copies = []
    for j in range(chunks):
        part = pl.ds(j * size, size)
        copy = remote(x_ref.at[part], pair_ref.at[core, part], send.at[j], recv.at[j], sibling)
        copy.start()
        copies.append(copy)
    through_vmem(x_ref, pair_ref.at[core], held, local)
    for copy in copies:
        copy.wait()


def start_scatter(cols, part_ref, got_ref, send, recv):
    row, col = place()
    copies = []
    for k in range(1, cols):
        dest = (col + k) % cols
        copy = remote(part_ref.at[dest], got_ref.at[k], send.at[k], recv.at[k], (row, dest))
        copy.start()
        copies.append(copy)
    return copies


def rows_kernel(
    cols, chunks, pair_ref, part_ref, all_ref, got_ref,
    y_send, y_recv, f_send, f_recv, s_send, s_recv, local, held, small,
):
    row, col = place()
    core = row % 2
    across, sibling = (flip(row, 2), col), (flip(row, 1), col)
    greet([across, sibling] + [(row, (col + k) % cols) for k in range(1, cols)])
    size = pair_ref.shape[1] // chunks
    parts = [pl.ds(j * size, size) for j in range(chunks)]
    outgoing = []
    for j, part in enumerate(parts):
        copy = remote(
            pair_ref.at[core, part], all_ref.at[row, part], y_send.at[j], y_recv.at[j], across
        )
        copy.start()
        outgoing.append(copy)
    scatter = start_scatter(cols, part_ref, got_ref, s_send, s_recv)
    through_vmem(part_ref.at[col], got_ref.at[0], small, local)
    through_vmem(pair_ref, all_ref.at[pl.ds(row - core, 2)], held, local)
    forwards = []
    for j, part in enumerate(parts):
        outgoing[j].wait_recv()
        there = all_ref.at[flip(row, 2), part]
        copy = remote(there, there, f_send.at[j], f_recv.at[j], sibling)
        copy.start()
        forwards.append(copy)
    for copy in outgoing:
        copy.wait_send()
    for copy in scatter + forwards:
        copy.wait()


def gather(rows, cols, share_ref, all_ref, send, recv, local, held):
    row, col = place()
    side, across, sibling = (row, flip(col, 1)), (flip(row, 2), col), (flip(row, 1), col)
    group = cols // 2
    sent = []

    def push(src, r, c, peer):
        copy = remote(src, all_ref.at[r, c], send.at[len(sent)], recv.at[r, c], peer)
        copy.start()
        sent.append(copy)

    def arrived(r, c):
        slot = all_ref.at[r, c]
        remote(slot, slot, send.at[0], recv.at[r, c], sibling).wait_recv()

    def member(m):
        return ((col // 2 + m) % group) * 2 + col % 2

    for m in range(1, group):
        push(share_ref, row, col, (row, member(group - m)))
    push(share_ref, row, col, side)
    push(share_ref, row, col, across)
    push(share_ref, row, col, sibling)
    through_vmem(share_ref, all_ref.at[row, col], held, local)
    far = flip(row, 2)
    for m in range(1, group):
        c = member(m)
        arrived(row, c)
        for peer in (side, across, sibling):
            push(all_ref.at[row, c], row, c, peer)
    for m in range(group):
        c = flip(member(m), 1)
        arrived(row, c)
        if 2 * m < group:
            push(all_ref.at[row, c], row, c, across)
        push(all_ref.at[row, c], row, c, sibling)
        c = member(m)
        arrived(far, c)
        if 2 * m >= group:
            push(all_ref.at[far, c], far, c, side)
        push(all_ref.at[far, c], far, c, sibling)
    for m in range(group):
        c = flip(member(m), 1)
        arrived(far, c)
        push(all_ref.at[far, c], far, c, sibling)
    for r in (flip(row, 1), flip(flip(row, 1), 2)):
        for c in range(cols):
            arrived(r, c)
    for copy in sent:
        copy.wait_send()


def gather_sends(cols):
    group = cols // 2
    return (group - 1) + 3 + 3 * (group - 1) + 3 * group + group


def gather_peers(cols):
    row, col = place()
    return [(flip(row, 2), col), (flip(row, 1), col)] + [(row, (col + k) % cols) for k in range(1, cols)]


def both_kernel(rows, cols, part_ref, share_ref, got_ref, all_ref, s_send, s_recv, g_send, g_recv, local, small, held):
    greet(gather_peers(cols))
    scatter = start_scatter(cols, part_ref, got_ref, s_send, s_recv)
    through_vmem(part_ref.at[lax.axis_index("cols")], got_ref.at[0], small, local)
    gather(rows, cols, share_ref, all_ref, g_send, g_recv, local, held)
    for copy in scatter:
        copy.wait()


def gather_kernel(rows, cols, share_ref, all_ref, g_send, g_recv, local, held):
    greet(gather_peers(cols))
    gather(rows, cols, share_ref, all_ref, g_send, g_recv, local, held)


def poly_kernel(near_ref, cross_ref, poly_ref, gram_ref):
    block, tile = poly_ref.shape
    half, strip = block // 2, 128
    row, step = lax.axis_index("rows"), pl.program_id(0)

    @pl.when(step == 0)
    def _():
        def put(i, j, start, source):
            count = source.shape[0]
            gram_ref[pl.ds(i * block + start, count), pl.ds(j * block, block)] = source[...]
            if i != j:

                @pl.loop(0, block, step=strip)
                def _(at):
                    gram_ref[
                        pl.ds(pl.multiple_of(j * block + at, strip), strip), pl.ds(i * block + start, count)
                    ] = source[:, pl.ds(pl.multiple_of(at, strip), strip)].T

        for i in range(4):
            put(i, i, 0, near_ref.at[i, pl.ds(0, block)])
        for core in range(2):
            put(0, 1, core * half, near_ref.at[core, pl.ds(block, half)])
            put(2, 3, core * half, near_ref.at[2 + core, pl.ds(block, half)])
        for r, (i, j) in enumerate(((0, 2), (1, 3), (2, 1), (3, 0))):
            put(i, j, 0, cross_ref.at[r, pl.ds(0, block)])

    mine = pl.ds(pl.multiple_of(row * block, block), block)
    slab = pl.ds(pl.multiple_of(step * tile, tile), tile)
    square = jnp.dot(gram_ref[mine, :], gram_ref[:, slab], preferred_element_type=jnp.float32)
    gram = gram_ref[mine, slab].astype(jnp.float32)
    poly_ref[...] = (cubic_coef * gram + quintic_coef * square).astype(bf16)


def poly_rows(near, cross, block):
    rows = near.shape[0]
    full, tile = rows * block, 512

    def whole(array):
        return pl.BlockSpec(array.shape, lambda step: (0, 0, 0), pipeline_mode=pl.Buffered(1))

    return pl.pallas_call(
        poly_kernel,
        grid=(full // tile,),
        out_shape=jax.ShapeDtypeStruct((block, full), bf16),
        in_specs=[whole(near), whole(cross)],
        out_specs=pl.BlockSpec((block, tile), lambda step: (0, step)),
        scratch_shapes=[pltpu.VMEM((full, full), bf16)],
        compiler_params=pltpu.CompilerParams(vmem_limit_bytes=58 * 2**20),
    )(near, cross)


def call(kernel, ident, args, outs, sems, holds):
    return pl.pallas_call(
        kernel,
        out_shape=outs,
        in_specs=[ANY] * len(args),
        out_specs=[ANY] * len(outs),
        scratch_shapes=[pltpu.SemaphoreType.DMA(shape) for shape in sems]
        + [pltpu.VMEM(shape, bf16) for shape in holds],
        compiler_params=pltpu.CompilerParams(
            collective_id=ident, has_side_effects=True, vmem_limit_bytes=32 * 2**20
        ),
    )(*args)


def dot_rows(left, right):
    return lax.dot_general(
        left, right, (((1,), (1,)), ((), ())), preferred_element_type=jnp.float32
    )


def round_up(value, unit):
    return -(-value // unit) * unit


def chunked(tile, cols):
    count = round_up(-(-tile.shape[0] // cols), 16)
    tile = jnp.pad(tile, ((0, count * cols - tile.shape[0]), (0, 0)))
    return tile.reshape(cols, count, tile.shape[1])


def on_device(iterate):
    rows, cols = lax.axis_size("rows"), lax.axis_size("cols")
    row = lax.axis_index("rows")
    block, width = iterate.shape
    half = block // 2
    vocab = width * cols
    full = block * rows
    chunks = 8

    def shape(*dims):
        return jax.ShapeDtypeStruct(dims, bf16)

    (pair,) = call(
        functools.partial(pair_kernel, 4), 1, [iterate], [shape(2, block, width)],
        [(4,), (4,), ()], [(block, width)],
    )
    top = lax.dynamic_slice(pair, (0, (row % 2) * half, 0), (1, half, width))[0]
    near = jnp.concatenate(
        [dot_rows(iterate, iterate).astype(bf16), dot_rows(top, pair[1]).astype(bf16)], axis=0
    )
    near = chunked(near, cols)
    near_rows = near.shape[1]
    all_rows, got = call(
        functools.partial(rows_kernel, cols, chunks),
        2,
        [pair, near],
        [shape(rows, block, width), shape(cols, near_rows, block)],
        [(chunks,)] * 4 + [(cols,), (cols,), ()],
        [(2, block, width), (near_rows, block)],
    )

    def summed(parts):
        return (jnp.sum(parts.astype(jnp.float32), axis=0) / vocab).astype(bf16)

    near_share = summed(got)
    other = jnp.where(row < 2, row + 2, rows - 1 - row)
    cross = dot_rows(iterate, lax.dynamic_index_in_dim(all_rows, other, 0, keepdims=False)).astype(bf16)
    cross = chunked(cross, cols)
    cross_rows = cross.shape[1]
    sends = gather_sends(cols)
    got, near_all = call(
        functools.partial(both_kernel, rows, cols),
        3,
        [cross, near_share],
        [shape(cols, cross_rows, block), shape(rows, cols, near_rows, block)],
        [(cols,), (cols,), (sends,), (rows, cols), ()],
        [(cross_rows, block), (near_rows, block)],
    )
    (cross_all,) = call(
        functools.partial(gather_kernel, rows, cols),
        4,
        [summed(got)],
        [shape(rows, cols, cross_rows, block)],
        [(sends,), (rows, cols), ()],
        [(cross_rows, block)],
    )
    near_all = near_all.reshape(rows, cols * near_rows, block)
    cross_all = cross_all.reshape(rows, cols * cross_rows, block)
    poly = poly_rows(near_all, cross_all, block)
    linear_part = linear_coef * iterate.astype(jnp.float32)
    mixed = linear_part + jnp.dot(
        poly, all_rows.reshape(full, width), preferred_element_type=jnp.float32
    )
    return mixed.astype(bf16)


def solution(mesh):
    return jax.shard_map(
        on_device,
        mesh=mesh,
        in_specs=(P("rows", "cols"),),
        out_specs=P("rows", "cols"),
        check_vma=False,
    )
```

```python
import functools

import jax
import jax.numpy as jnp
from jax import lax
from jax.experimental import pallas as pl
from jax.experimental.pallas import tpu as pltpu
from jax.sharding import PartitionSpec as P

linear_coef = 3.4445
cubic_coef = -4.775
quintic_coef = 2.0315

MESH = pl.DeviceIdType.MESH
ANY = pl.BlockSpec(memory_space=pl.ANY)
bf16 = jnp.bfloat16


def greet(peers):
    barrier = pltpu.get_barrier_semaphore()
    for peer in peers:
        pl.semaphore_signal(barrier, inc=1, device_id=peer, device_id_type=MESH)
    pl.semaphore_wait(barrier, len(peers))


def remote(src, dst, send, recv, peer):
    return pltpu.make_async_remote_copy(
        src_ref=src, dst_ref=dst, send_sem=send, recv_sem=recv, device_id=peer, device_id_type=MESH
    )


def flip(index, bit):
    return index + bit - 2 * bit * ((index // bit) % 2)


def place():
    row, col = lax.axis_index("rows"), lax.axis_index("cols")
    return row, col


def through_vmem(src, dst, held, sem):
    for a, b in ((src, held), (held, dst)):
        copy = pltpu.make_async_copy(a, b, sem)
        copy.start()
        copy.wait()


def pair_kernel(chunks, x_ref, pair_ref, send, recv, local, held):
    row, col = place()
    sibling = (flip(row, 1), col)
    core = row % 2
    greet([sibling])
    size = x_ref.shape[0] // chunks
    copies = []
    for j in range(chunks):
        part = pl.ds(j * size, size)
        copy = remote(x_ref.at[part], pair_ref.at[core, part], send.at[j], recv.at[j], sibling)
        copy.start()
        copies.append(copy)
    through_vmem(x_ref, pair_ref.at[core], held, local)
    for copy in copies:
        copy.wait()


def start_scatter(cols, part_ref, got_ref, send, recv):
    row, col = place()
    copies = []
    for k in range(1, cols):
        dest = (col + k) % cols
        copy = remote(part_ref.at[dest], got_ref.at[k], send.at[k], recv.at[k], (row, dest))
        copy.start()
        copies.append(copy)
    return copies


def rows_kernel(
    cols, chunks, vocab, pair_ref, part_ref, all_ref, near_ref,
    y_send, y_recv, f_send, f_recv, s_send, s_recv, g_send, g_recv, local, held, parts_held, share_held,
):
    row, col = place()
    core = row % 2
    across, sibling, side = (flip(row, 2), col), (flip(row, 1), col), (row, flip(col, 1))
    greet([across, sibling] + [(row, (col + k) % cols) for k in range(1, cols)])
    size = pair_ref.shape[1] // chunks
    parts = [pl.ds(j * size, size) for j in range(chunks)]
    outgoing = []
    for j, part in enumerate(parts):
        copy = remote(
            pair_ref.at[core, part], all_ref.at[row, part], y_send.at[j], y_recv.at[j], across
        )
        copy.start()
        outgoing.append(copy)
    scatter = start_scatter(cols, part_ref, parts_held, s_send, s_recv)
    mine = pltpu.make_async_copy(part_ref.at[col], parts_held.at[0], local)
    mine.start()
    mine.wait()
    through_vmem(pair_ref, all_ref.at[pl.ds(row - core, 2)], held, local)
    for copy in scatter:
        copy.wait()

    @pl.loop(0, share_held.shape[0], step=16)
    def _(at):
        band = pl.ds(pl.multiple_of(at, 16), 16)
        total = parts_held[0, band, :].astype(jnp.float32)
        for k in range(1, cols):
            total = total + parts_held[k, band, :].astype(jnp.float32)
        share_held[band, :] = (total / vocab).astype(bf16)

    group = cols // 2
    sent = []

    def push(src, c, peer):
        copy = remote(src, near_ref.at[row, c], g_send.at[len(sent)], g_recv.at[row % 2, c], peer)
        copy.start()
        sent.append(copy)

    def arrived(r, c):
        slot = near_ref.at[r, c]
        remote(slot, slot, g_send.at[0], g_recv.at[r % 2, c], sibling).wait_recv()

    def member(m):
        return ((col // 2 + m) % group) * 2 + col % 2

    for m in range(1, group):
        push(share_held, col, (row, member(group - m)))
    push(share_held, col, side)
    push(share_held, col, sibling)
    keep = pltpu.make_async_copy(share_held, near_ref.at[row, col], local)
    keep.start()
    keep.wait()
    forwards = []

    def forward(j):
        outgoing[j].wait_recv()
        there = all_ref.at[flip(row, 2), parts[j]]
        copy = remote(there, there, f_send.at[j], f_recv.at[j], sibling)
        copy.start()
        forwards.append(copy)

    early = chunks * 3 // 4
    for j in range(early):
        forward(j)
    for m in range(1, group):
        c = member(m)
        arrived(row, c)
        push(near_ref.at[row, c], c, side)
        push(near_ref.at[row, c], c, sibling)
    for j in range(early, chunks):
        forward(j)
    for m in range(group):
        c = flip(member(m), 1)
        arrived(row, c)
        push(near_ref.at[row, c], c, sibling)
    for c in range(cols):
        arrived(flip(row, 1), c)
    for copy in outgoing + sent:
        copy.wait_send()
    for copy in forwards:
        copy.wait()


def gather(rows, cols, share_ref, all_ref, send, recv, local, held):
    row, col = place()
    side, across, sibling = (row, flip(col, 1)), (flip(row, 2), col), (flip(row, 1), col)
    group = cols // 2
    sent = []

    def push(src, r, c, peer):
        copy = remote(src, all_ref.at[r, c], send.at[len(sent)], recv.at[r, c], peer)
        copy.start()
        sent.append(copy)

    def arrived(r, c):
        slot = all_ref.at[r, c]
        remote(slot, slot, send.at[0], recv.at[r, c], sibling).wait_recv()

    def member(m):
        return ((col // 2 + m) % group) * 2 + col % 2

    for m in range(1, group):
        push(share_ref, row, col, (row, member(group - m)))
    push(share_ref, row, col, side)
    push(share_ref, row, col, across)
    push(share_ref, row, col, sibling)
    through_vmem(share_ref, all_ref.at[row, col], held, local)
    far = flip(row, 2)
    for m in range(1, group):
        c = member(m)
        arrived(row, c)
        for peer in (side, across, sibling):
            push(all_ref.at[row, c], row, c, peer)
    for m in range(group):
        c = flip(member(m), 1)
        arrived(row, c)
        if 2 * m < group:
            push(all_ref.at[row, c], row, c, across)
        push(all_ref.at[row, c], row, c, sibling)
        c = member(m)
        arrived(far, c)
        if 2 * m >= group:
            push(all_ref.at[far, c], far, c, side)
        push(all_ref.at[far, c], far, c, sibling)
    for m in range(group):
        c = flip(member(m), 1)
        arrived(far, c)
        push(all_ref.at[far, c], far, c, sibling)
    for r in (flip(row, 1), flip(flip(row, 1), 2)):
        for c in range(cols):
            arrived(r, c)
    for copy in sent:
        copy.wait_send()


def gather_sends(cols):
    group = cols // 2
    return (group - 1) + 3 + 3 * (group - 1) + 3 * group + group


def gather_peers(cols):
    row, col = place()
    return [(flip(row, 2), col), (flip(row, 1), col)] + [(row, (col + k) % cols) for k in range(1, cols)]


def both_kernel(rows, cols, part_ref, plane_ref, got_ref, near_ref, s_send, s_recv, g_send, g_recv, local, small):
    row, col = place()
    across, sibling = (flip(row, 2), col), (flip(row, 1), col)
    greet(gather_peers(cols))
    copies = []
    for c in range(cols):
        slot = near_ref.at[row, c]
        copy = remote(slot, slot, g_send.at[0, c], g_recv.at[0, c], across)
        copy.start()
        copies.append(copy)
    scatter = start_scatter(cols, part_ref, got_ref, s_send, s_recv)
    through_vmem(part_ref.at[col], got_ref.at[0], small, local)
    for c in range(cols):
        copies[c].wait_recv()
        slot = near_ref.at[flip(row, 2), c]
        copy = remote(slot, slot, g_send.at[1, c], g_recv.at[1, c], sibling)
        copy.start()
        copies.append(copy)
    for copy in copies[:cols]:
        copy.wait_send()
    for copy in copies[cols:] + scatter:
        copy.wait()


def gather_kernel(rows, cols, share_ref, all_ref, g_send, g_recv, local, held):
    greet(gather_peers(cols))
    gather(rows, cols, share_ref, all_ref, g_send, g_recv, local, held)


def poly_kernel(near_ref, cross_ref, poly_ref, gram_ref):
    block, tile = poly_ref.shape
    half, strip = block // 2, 128
    row, step = lax.axis_index("rows"), pl.program_id(0)

    @pl.when(step == 0)
    def _():
        def put(i, j, start, source):
            count = source.shape[0]
            gram_ref[pl.ds(i * block + start, count), pl.ds(j * block, block)] = source[...]
            if i != j:

                @pl.loop(0, block, step=strip)
                def _(at):
                    gram_ref[
                        pl.ds(pl.multiple_of(j * block + at, strip), strip), pl.ds(i * block + start, count)
                    ] = source[:, pl.ds(pl.multiple_of(at, strip), strip)].T

        for i in range(4):
            put(i, i, 0, near_ref.at[i, pl.ds(0, block)])
        for core in range(2):
            put(0, 1, core * half, near_ref.at[core, pl.ds(block, half)])
            put(2, 3, core * half, near_ref.at[2 + core, pl.ds(block, half)])
        for r, (i, j) in enumerate(((0, 2), (1, 3), (2, 1), (3, 0))):
            put(i, j, 0, cross_ref.at[r, pl.ds(0, block)])

    mine = pl.ds(pl.multiple_of(row * block, block), block)
    slab = pl.ds(pl.multiple_of(step * tile, tile), tile)
    square = jnp.dot(gram_ref[mine, :], gram_ref[:, slab], preferred_element_type=jnp.float32)
    gram = gram_ref[mine, slab].astype(jnp.float32)
    poly_ref[...] = (cubic_coef * gram + quintic_coef * square).astype(bf16)


def poly_rows(near, cross, block):
    rows = near.shape[0]
    full, tile = rows * block, 512

    def whole(array):
        return pl.BlockSpec(array.shape, lambda step: (0, 0, 0), pipeline_mode=pl.Buffered(1))

    return pl.pallas_call(
        poly_kernel,
        grid=(full // tile,),
        out_shape=jax.ShapeDtypeStruct((block, full), bf16),
        in_specs=[whole(near), whole(cross)],
        out_specs=pl.BlockSpec((block, tile), lambda step: (0, step)),
        scratch_shapes=[pltpu.VMEM((full, full), bf16)],
        compiler_params=pltpu.CompilerParams(vmem_limit_bytes=58 * 2**20),
    )(near, cross)


def call(kernel, ident, args, outs, sems, holds, alias={}):
    return pl.pallas_call(
        kernel,
        out_shape=outs,
        in_specs=[ANY] * len(args),
        out_specs=[ANY] * len(outs),
        input_output_aliases=alias,
        scratch_shapes=[pltpu.SemaphoreType.DMA(shape) for shape in sems]
        + [pltpu.VMEM(shape, bf16) for shape in holds],
        compiler_params=pltpu.CompilerParams(
            collective_id=ident, has_side_effects=True, vmem_limit_bytes=32 * 2**20
        ),
    )(*args)


def dot_rows(left, right):
    return lax.dot_general(
        left, right, (((1,), (1,)), ((), ())), preferred_element_type=jnp.float32
    )


def round_up(value, unit):
    return -(-value // unit) * unit


def chunked(tile, cols):
    count = round_up(-(-tile.shape[0] // cols), 16)
    tile = jnp.pad(tile, ((0, count * cols - tile.shape[0]), (0, 0)))
    return tile.reshape(cols, count, tile.shape[1])


def on_device(iterate):
    rows, cols = lax.axis_size("rows"), lax.axis_size("cols")
    row = lax.axis_index("rows")
    block, width = iterate.shape
    half = block // 2
    vocab = width * cols
    full = block * rows
    chunks = 8

    def shape(*dims):
        return jax.ShapeDtypeStruct(dims, bf16)

    (pair,) = call(
        functools.partial(pair_kernel, 4), 1, [iterate], [shape(2, block, width)],
        [(4,), (4,), ()], [(block, width)],
    )
    top = lax.dynamic_slice(pair, (0, (row % 2) * half, 0), (1, half, width))[0]
    near = jnp.concatenate(
        [dot_rows(iterate, iterate).astype(bf16), dot_rows(top, pair[1]).astype(bf16)], axis=0
    )
    near = chunked(near, cols)
    near_rows = near.shape[1]
    sends = gather_sends(cols)
    all_rows, near_all = call(
        functools.partial(rows_kernel, cols, chunks, vocab),
        2,
        [pair, near],
        [shape(rows, block, width), shape(rows, cols, near_rows, block)],
        [(chunks,)] * 4 + [(cols,), (cols,), (sends,), (2, cols), ()],
        [(2, block, width), (cols, near_rows, block), (near_rows, block)],
    )

    def summed(parts):
        return (jnp.sum(parts.astype(jnp.float32), axis=0) / vocab).astype(bf16)

    other = jnp.where(row < 2, row + 2, rows - 1 - row)
    cross = dot_rows(iterate, lax.dynamic_index_in_dim(all_rows, other, 0, keepdims=False)).astype(bf16)
    cross = chunked(cross, cols)
    cross_rows = cross.shape[1]
    got, near_all = call(
        functools.partial(both_kernel, rows, cols),
        3,
        [cross, near_all],
        [shape(cols, cross_rows, block), shape(rows, cols, near_rows, block)],
        [(cols,), (cols,), (2, cols), (2, cols), ()],
        [(cross_rows, block)],
        {1: 1},
    )
    (cross_all,) = call(
        functools.partial(gather_kernel, rows, cols),
        4,
        [summed(got)],
        [shape(rows, cols, cross_rows, block)],
        [(sends,), (rows, cols), ()],
        [(cross_rows, block)],
    )
    near_all = near_all.reshape(rows, cols * near_rows, block)
    cross_all = cross_all.reshape(rows, cols * cross_rows, block)
    poly = poly_rows(near_all, cross_all, block)
    linear_part = linear_coef * iterate.astype(jnp.float32)
    mixed = linear_part + jnp.dot(
        poly, all_rows.reshape(full, width), preferred_element_type=jnp.float32
    )
    return mixed.astype(bf16)


def solution(mesh):
    return jax.shard_map(
        on_device,
        mesh=mesh,
        in_specs=(P("rows", "cols"),),
        out_specs=P("rows", "cols"),
        check_vma=False,
    )
```

```python
import functools

import jax
import jax.numpy as jnp
from jax import lax
from jax.experimental import pallas as pl
from jax.experimental.pallas import tpu as pltpu
from jax.sharding import PartitionSpec as P

linear_coef = 3.4445
cubic_coef = -4.775
quintic_coef = 2.0315

MESH = pl.DeviceIdType.MESH
ANY = pl.BlockSpec(memory_space=pl.ANY)
bf16 = jnp.bfloat16


def greet(peers):
    barrier = pltpu.get_barrier_semaphore()
    for peer in peers:
        pl.semaphore_signal(barrier, inc=1, device_id=peer, device_id_type=MESH)
    pl.semaphore_wait(barrier, len(peers))


def remote(src, dst, send, recv, peer):
    return pltpu.make_async_remote_copy(
        src_ref=src, dst_ref=dst, send_sem=send, recv_sem=recv, device_id=peer, device_id_type=MESH
    )


def flip(index, bit):
    return index + bit - 2 * bit * ((index // bit) % 2)


def place():
    row, col = lax.axis_index("rows"), lax.axis_index("cols")
    return row, col


def through_vmem(src, dst, held, sem):
    for a, b in ((src, held), (held, dst)):
        copy = pltpu.make_async_copy(a, b, sem)
        copy.start()
        copy.wait()


def pair_kernel(chunks, x_ref, pair_ref, send, recv, local, held):
    row, col = place()
    sibling = (flip(row, 1), col)
    core = row % 2
    greet([sibling])
    size = x_ref.shape[0] // chunks
    copies = []
    for j in range(chunks):
        part = pl.ds(j * size, size)
        copy = remote(x_ref.at[part], pair_ref.at[core, part], send.at[j], recv.at[j], sibling)
        copy.start()
        copies.append(copy)
    through_vmem(x_ref, pair_ref.at[core], held, local)
    for copy in copies:
        copy.wait()


def start_scatter(cols, part_ref, got_ref, send, recv):
    row, col = place()
    copies = []
    for k in range(1, cols):
        dest = (col + k) % cols
        copy = remote(part_ref.at[dest], got_ref.at[k], send.at[k], recv.at[k], (row, dest))
        copy.start()
        copies.append(copy)
    return copies


def rows_kernel(
    cols, chunks, vocab, pair_ref, part_ref, all_ref, near_ref,
    y_send, y_recv, f_send, f_recv, s_send, s_recv, g_send, g_recv, local, held, parts_held, share_held,
):
    row, col = place()
    core = row % 2
    across, sibling, side = (flip(row, 2), col), (flip(row, 1), col), (row, flip(col, 1))
    greet([across, sibling] + [(row, (col + k) % cols) for k in range(1, cols)])
    size = pair_ref.shape[1] // chunks
    parts = [pl.ds(j * size, size) for j in range(chunks)]
    outgoing = []
    for j, part in enumerate(parts):
        copy = remote(
            pair_ref.at[core, part], all_ref.at[row, part], y_send.at[j], y_recv.at[j], across
        )
        copy.start()
        outgoing.append(copy)
    scatter = start_scatter(cols, part_ref, parts_held, s_send, s_recv)
    mine = pltpu.make_async_copy(part_ref.at[col], parts_held.at[0], local)
    mine.start()
    mine.wait()
    through_vmem(pair_ref, all_ref.at[pl.ds(row - core, 2)], held, local)
    for copy in scatter:
        copy.wait()

    @pl.loop(0, share_held.shape[0], step=16)
    def _(at):
        band = pl.ds(pl.multiple_of(at, 16), 16)
        total = parts_held[0, band, :].astype(jnp.float32)
        for k in range(1, cols):
            total = total + parts_held[k, band, :].astype(jnp.float32)
        share_held[band, :] = (total / vocab).astype(bf16)

    group = cols // 2
    sent = []

    def push(src, c, peer):
        copy = remote(src, near_ref.at[row, c], g_send.at[len(sent)], g_recv.at[row % 2, c], peer)
        copy.start()
        sent.append(copy)

    def arrived(r, c):
        slot = near_ref.at[r, c]
        remote(slot, slot, g_send.at[0], g_recv.at[r % 2, c], sibling).wait_recv()

    def member(m):
        return ((col // 2 + m) % group) * 2 + col % 2

    for m in range(1, group):
        push(share_held, col, (row, member(group - m)))
    push(share_held, col, side)
    push(share_held, col, sibling)
    keep = pltpu.make_async_copy(share_held, near_ref.at[row, col], local)
    keep.start()
    keep.wait()
    forwards = []

    def forward(j):
        outgoing[j].wait_recv()
        there = all_ref.at[flip(row, 2), parts[j]]
        copy = remote(there, there, f_send.at[j], f_recv.at[j], sibling)
        copy.start()
        forwards.append(copy)

    early = chunks * 3 // 4
    for j in range(early):
        forward(j)
    for m in range(1, group):
        c = member(m)
        arrived(row, c)
        push(near_ref.at[row, c], c, side)
        push(near_ref.at[row, c], c, sibling)
    for j in range(early, chunks):
        forward(j)
    for m in range(group):
        c = flip(member(m), 1)
        arrived(row, c)
        push(near_ref.at[row, c], c, sibling)
    for c in range(cols):
        arrived(flip(row, 1), c)
    for copy in outgoing + sent:
        copy.wait_send()
    for copy in forwards:
        copy.wait()


def gather(rows, cols, share_ref, all_ref, send, recv, local, held):
    row, col = place()
    side, across, sibling = (row, flip(col, 1)), (flip(row, 2), col), (flip(row, 1), col)
    group = cols // 2
    sent = []

    def push(src, r, c, peer):
        copy = remote(src, all_ref.at[r, c], send.at[len(sent)], recv.at[r, c], peer)
        copy.start()
        sent.append(copy)

    def arrived(r, c):
        slot = all_ref.at[r, c]
        remote(slot, slot, send.at[0], recv.at[r, c], sibling).wait_recv()

    def member(m):
        return ((col // 2 + m) % group) * 2 + col % 2

    for m in range(1, group):
        push(share_ref, row, col, (row, member(group - m)))
    push(share_ref, row, col, side)
    push(share_ref, row, col, across)
    push(share_ref, row, col, sibling)
    through_vmem(share_ref, all_ref.at[row, col], held, local)
    far = flip(row, 2)
    for m in range(1, group):
        c = member(m)
        arrived(row, c)
        for peer in (side, across, sibling):
            push(all_ref.at[row, c], row, c, peer)
    for m in range(group):
        c = flip(member(m), 1)
        arrived(row, c)
        if 2 * m < group:
            push(all_ref.at[row, c], row, c, across)
        push(all_ref.at[row, c], row, c, sibling)
        c = member(m)
        arrived(far, c)
        if 2 * m >= group:
            push(all_ref.at[far, c], far, c, side)
        push(all_ref.at[far, c], far, c, sibling)
    for m in range(group):
        c = flip(member(m), 1)
        arrived(far, c)
        push(all_ref.at[far, c], far, c, sibling)
    for r in (flip(row, 1), flip(flip(row, 1), 2)):
        for c in range(cols):
            arrived(r, c)
    for copy in sent:
        copy.wait_send()


def gather_sends(cols):
    group = cols // 2
    return (group - 1) + 3 + 3 * (group - 1) + 3 * group + group


def gather_peers(cols):
    row, col = place()
    return [(flip(row, 2), col), (flip(row, 1), col)] + [(row, (col + k) % cols) for k in range(1, cols)]


def both_kernel(rows, cols, part_ref, plane_ref, got_ref, near_ref, s_send, s_recv, g_send, g_recv, local, small):
    row, col = place()
    across, sibling = (flip(row, 2), col), (flip(row, 1), col)
    greet(gather_peers(cols))
    side, far, group = (row, flip(col, 1)), flip(row, 2), cols // 2
    members = [((col // 2 + m) % group) * 2 + col % 2 for m in range(group)]
    cut = group // 2
    shared = group - cut

    def push(r, c, send_at, recv_at, peer):
        slot = near_ref.at[r, c]
        copy = remote(slot, slot, g_send.at[send_at, c], g_recv.at[recv_at, c], peer)
        copy.start()
        return copy

    order = members[cut:] + members[:cut] + [flip(c, 1) for c in members[:cut]]
    direct = [push(row, c, 0, 0, across) for c in order]
    scatter = start_scatter(cols, part_ref, got_ref, s_send, s_recv)
    through_vmem(part_ref.at[col], got_ref.at[0], small, local)
    passed, forwards = [], []
    for k, c in enumerate(order):
        direct[k].wait_recv()
        if k < shared:
            passed.append(push(far, c, 2, 0, side))
        forwards.append(push(far, c, 1, 1, sibling))
    for c in members[cut:]:
        c = flip(c, 1)
        slot = near_ref.at[far, c]
        remote(slot, slot, g_send.at[0, c], g_recv.at[0, c], side).wait_recv()
        forwards.append(push(far, c, 1, 1, sibling))
    for copy in direct + passed:
        copy.wait_send()
    for copy in forwards + scatter:
        copy.wait()


def gather_kernel(rows, cols, share_ref, all_ref, g_send, g_recv, local, held):
    greet(gather_peers(cols))
    gather(rows, cols, share_ref, all_ref, g_send, g_recv, local, held)


def poly_kernel(near_ref, cross_ref, poly_ref, gram_ref):
    block, tile = poly_ref.shape
    half, strip = block // 2, 128
    row, step = lax.axis_index("rows"), pl.program_id(0)

    @pl.when(step == 0)
    def _():
        def put(i, j, start, source):
            count = source.shape[0]
            gram_ref[pl.ds(i * block + start, count), pl.ds(j * block, block)] = source[...]
            if i != j:

                @pl.loop(0, block, step=strip)
                def _(at):
                    gram_ref[
                        pl.ds(pl.multiple_of(j * block + at, strip), strip), pl.ds(i * block + start, count)
                    ] = source[:, pl.ds(pl.multiple_of(at, strip), strip)].T

        for i in range(4):
            put(i, i, 0, near_ref.at[i, pl.ds(0, block)])
        for core in range(2):
            put(0, 1, core * half, near_ref.at[core, pl.ds(block, half)])
            put(2, 3, core * half, near_ref.at[2 + core, pl.ds(block, half)])
        for r, (i, j) in enumerate(((0, 2), (1, 3), (2, 1), (3, 0))):
            put(i, j, 0, cross_ref.at[r, pl.ds(0, block)])

    mine = pl.ds(pl.multiple_of(row * block, block), block)
    slab = pl.ds(pl.multiple_of(step * tile, tile), tile)
    square = jnp.dot(gram_ref[mine, :], gram_ref[:, slab], preferred_element_type=jnp.float32)
    gram = gram_ref[mine, slab].astype(jnp.float32)
    poly_ref[...] = (cubic_coef * gram + quintic_coef * square).astype(bf16)


def poly_rows(near, cross, block):
    rows = near.shape[0]
    full, tile = rows * block, 512

    def whole(array):
        return pl.BlockSpec(array.shape, lambda step: (0, 0, 0), pipeline_mode=pl.Buffered(1))

    return pl.pallas_call(
        poly_kernel,
        grid=(full // tile,),
        out_shape=jax.ShapeDtypeStruct((block, full), bf16),
        in_specs=[whole(near), whole(cross)],
        out_specs=pl.BlockSpec((block, tile), lambda step: (0, step)),
        scratch_shapes=[pltpu.VMEM((full, full), bf16)],
        compiler_params=pltpu.CompilerParams(vmem_limit_bytes=58 * 2**20),
    )(near, cross)


def call(kernel, ident, args, outs, sems, holds, alias={}):
    return pl.pallas_call(
        kernel,
        out_shape=outs,
        in_specs=[ANY] * len(args),
        out_specs=[ANY] * len(outs),
        input_output_aliases=alias,
        scratch_shapes=[pltpu.SemaphoreType.DMA(shape) for shape in sems]
        + [pltpu.VMEM(shape, bf16) for shape in holds],
        compiler_params=pltpu.CompilerParams(
            collective_id=ident, has_side_effects=True, vmem_limit_bytes=32 * 2**20
        ),
    )(*args)


def dot_rows(left, right):
    return lax.dot_general(
        left, right, (((1,), (1,)), ((), ())), preferred_element_type=jnp.float32
    )


def round_up(value, unit):
    return -(-value // unit) * unit


def chunked(tile, cols):
    count = round_up(-(-tile.shape[0] // cols), 16)
    tile = jnp.pad(tile, ((0, count * cols - tile.shape[0]), (0, 0)))
    return tile.reshape(cols, count, tile.shape[1])


def on_device(iterate):
    rows, cols = lax.axis_size("rows"), lax.axis_size("cols")
    row = lax.axis_index("rows")
    block, width = iterate.shape
    half = block // 2
    vocab = width * cols
    full = block * rows
    chunks = 8

    def shape(*dims):
        return jax.ShapeDtypeStruct(dims, bf16)

    (pair,) = call(
        functools.partial(pair_kernel, 4), 1, [iterate], [shape(2, block, width)],
        [(4,), (4,), ()], [(block, width)],
    )
    top = lax.dynamic_slice(pair, (0, (row % 2) * half, 0), (1, half, width))[0]
    near = jnp.concatenate(
        [dot_rows(iterate, iterate).astype(bf16), dot_rows(top, pair[1]).astype(bf16)], axis=0
    )
    near = chunked(near, cols)
    near_rows = near.shape[1]
    sends = gather_sends(cols)
    all_rows, near_all = call(
        functools.partial(rows_kernel, cols, chunks, vocab),
        2,
        [pair, near],
        [shape(rows, block, width), shape(rows, cols, near_rows, block)],
        [(chunks,)] * 4 + [(cols,), (cols,), (sends,), (2, cols), ()],
        [(2, block, width), (cols, near_rows, block), (near_rows, block)],
    )

    def summed(parts):
        return (jnp.sum(parts.astype(jnp.float32), axis=0) / vocab).astype(bf16)

    other = jnp.where(row < 2, row + 2, rows - 1 - row)
    cross = dot_rows(iterate, lax.dynamic_index_in_dim(all_rows, other, 0, keepdims=False)).astype(bf16)
    cross = chunked(cross, cols)
    cross_rows = cross.shape[1]
    got, near_all = call(
        functools.partial(both_kernel, rows, cols),
        3,
        [cross, near_all],
        [shape(cols, cross_rows, block), shape(rows, cols, near_rows, block)],
        [(cols,), (cols,), (3, cols), (2, cols), ()],
        [(cross_rows, block)],
        {1: 1},
    )
    (cross_all,) = call(
        functools.partial(gather_kernel, rows, cols),
        4,
        [summed(got)],
        [shape(rows, cols, cross_rows, block)],
        [(sends,), (rows, cols), ()],
        [(cross_rows, block)],
    )
    near_all = near_all.reshape(rows, cols * near_rows, block)
    cross_all = cross_all.reshape(rows, cols * cross_rows, block)
    poly = poly_rows(near_all, cross_all, block)
    linear_part = linear_coef * iterate.astype(jnp.float32)
    mixed = linear_part + jnp.dot(
        poly, all_rows.reshape(full, width), preferred_element_type=jnp.float32
    )
    return mixed.astype(bf16)


def solution(mesh):
    return jax.shard_map(
        on_device,
        mesh=mesh,
        in_specs=(P("rows", "cols"),),
        out_specs=P("rows", "cols"),
        check_vma=False,
    )
```
